32 devices in a mesh: grp: 2 (over y), wide: 8 (over z, x), narrow: 2 (over core).
Axes of the slice: x: 2, y: 2, z: 4, core: 2. Of those that a mesh axis runs over, the one named last changes fastest.
Arguments:
- traces: bfloat16 [1024, 64, 512], P('wide', ('grp', 'narrow')), parts along dimension 1, may hold values from -6 to 6
- aperture: int32 [64, 1], P(('grp', 'narrow')), parts along dimension 0, may hold values 0 or 1
- source_points: int32 [64], P('grp'), parts along dimension 0, may hold values from 0 to 511, as said below
- freq_idx: int32 [2], replicated, may hold values from 1 to 511
Outputs:
- multiples: float32 [2, 2, 64, 512], P(None, None, ('grp', 'narrow'), 'wide'), parts along dimension 2
The draws below stay inside these ranges and needn't reach their ends.
There are 2 independent parts, one for each index of `grp`. The reference program is written for one: setup_inputs(seed, part) draws one part's arguments, and reference() takes and returns one part's arrays. A program takes and returns all parts, laid end to end along the dimension named above; an argument that names none is the same for every part. Nothing has to cross between parts.
Inputs may be any that keep to these rules, and one draw needn't show every extreme that they name: `source_points`: shot k stands at a receiver of k * 16 to (k + 1) * 16 - 1; the first shot at receiver 0 and the last at receiver 512 - 1.
All inputs are finite; a program needn't handle non-finite values. No bound on the sum of `aperture` on one device may be relied on, other than what follows from the above.
Results may differ from the reference program's by a relative error of at most 0.0033.
Values may be sent and summed in bfloat16 or wider, within the bound.
A program may use at most 192 MiB of HBM per device.

```python
import math
import jax
import jax.numpy as jnp
from jax import lax

NT = 1024
FREQS = 2
RB = 512
S = 32
K = 512
KB = 1


def draw_source_points(key, part):
    key = jax.random.fold_in(key, 7)
    span_width = K // S
    offsets = jax.random.randint(key, (S,), 0, span_width)
    offsets = offsets.at[0].set(0).at[S - 1].set(span_width - 1)
    return (jnp.arange(S, dtype=jnp.int32) * span_width + offsets).astype(jnp.int32)


def with_ends(entries, key, smallest, largest):
    spot = [jax.random.randint(jax.random.fold_in(key, axis), (), 0, length) for axis, length in enumerate(entries.shape)]
    widest = entries.shape.index(max(entries.shape))
    beside = spot[:widest] + [(spot[widest] + 1) % entries.shape[widest]] + spot[widest + 1:]
    return entries.at[tuple(spot)].set(smallest).at[tuple(beside)].set(largest)


def steps_of(stream_key, extent, shards, least, top_value):
    def one(dim, shards_of):
        draws = jax.random.uniform(jax.random.fold_in(jax.random.fold_in(stream_key, 6), dim), (shards_of,), jnp.float32, least / len(shards), top_value / len(shards))
        return jnp.repeat(jnp.exp(draws), extent[dim] // shards_of).reshape((-1,) + (1,) * (len(extent) - dim - 1))

    gain = one(*shards[0])
    for cut in shards[1:]:
        gain = gain * one(*cut)
    return gain


def normal_values(key, shape, deviation, limit, pieces=(), kind=jnp.bfloat16):
    gain = steps_of(key, shape, pieces, -0.22, 0.18) if pieces else 1.0
    result = jax.random.normal(key, shape, jnp.float32) * deviation * gain
    return jnp.minimum(jnp.maximum(result, -limit), limit).astype(kind)


def setup_inputs(seed: int = 0, part: int = 0) -> dict:
    keys = jax.random.split(jax.random.key(seed), 5)
    part_splits = jax.random.split(jax.random.fold_in(keys[4], part), 5)
    traces = normal_values(part_splits[0], (NT, S, K), 1.0, 6.0, ((0, 8), (1, 2)))
    aperture = with_ends((jax.random.randint(part_splits[1], (S, KB), 0, 4) < 3).astype(jnp.int32), jax.random.fold_in(part_splits[1], 1), 0, 1)
    source_points = draw_source_points(jax.random.fold_in(jax.random.fold_in(keys[4], part), 71), part)
    freq_idx = jax.random.randint(keys[3], (FREQS,), 1, NT // 2).astype(jnp.int32)
    return {"traces": traces, "aperture": aperture, "source_points": source_points, "freq_idx": freq_idx}


def dft_rows(time_samples_count, freq_rows):
    phase_index = (freq_rows[:, None] * time_samples_count[None, :]) % NT
    angles = (2.0 * math.pi / NT) * phase_index.astype(jnp.float32)
    return jnp.concatenate([jnp.cos(angles), -jnp.sin(angles)], axis=0).astype(jnp.bfloat16)


def product_mix(left_side, right_side):
    return jnp.einsum("qsk,qkr->qsr", left_side, right_side, precision=lax.Precision.HIGHEST)


def reference(traces, aperture, source_points, freq_idx):
    fourier_table = dft_rows(jnp.arange(NT, dtype=jnp.int32), freq_idx)

    def one_shot(shot_index):
        shot_traces = lax.dynamic_index_in_dim(traces, shot_index, 1, keepdims=False)
        return jnp.dot(fourier_table, shot_traces, preferred_element_type=jnp.float32)

    raw_spectra = lax.map(one_shot, jnp.arange(S, dtype=jnp.int32))
    spectra = jnp.transpose(raw_spectra, (1, 0, 2)).reshape(2, FREQS, S, K)
    blocks = jnp.arange(K, dtype=jnp.int32) // RB
    active_mask = jnp.take(aperture, blocks, axis=1).astype(jnp.float32)
    spectra = spectra * active_mask * (NT ** -0.5)
    coincident = jnp.take(spectra, source_points, axis=3)
    real_part = product_mix(coincident[0], spectra[0]) - product_mix(coincident[1], spectra[1])
    imag_part = product_mix(coincident[0], spectra[1]) + product_mix(coincident[1], spectra[0])
    return jnp.stack([real_part, imag_part]) * (S ** -0.5)
```

```python
import functools
import math

import jax
import jax.numpy as jnp
from jax import lax
from jax.experimental import pallas as pl
from jax.experimental.pallas import tpu as pltpu
from jax.sharding import PartitionSpec as P

NT = 1024
RB = 512
LANES = 128
MESH = pl.DeviceIdType.MESH
F32 = jnp.float32
BF16 = jnp.bfloat16
SIN_TERMS = tuple((-1.0) ** i / math.factorial(2 * i + 1) for i in range(6))


def iota(shape, axis):
    return lax.broadcasted_iota(jnp.int32, shape, axis)


def each(count, body):
    if count <= 16:
        for i in range(count):
            body(i)
    else:
        lax.fori_loop(0, count, lambda i, c: (body(i), c)[1], 0)


def dft_block(freq_ref, first_time, shots, columns, first_column):
    shape = (8, columns)
    row = iota(shape, 0)
    lane = iota(shape, 1) + first_column
    freq = jnp.where(row % 2 == 0, freq_ref[0], freq_ref[1])
    m = freq * (first_time + lane // shots)
    m = (m + jnp.where(row >= 2, NT // 4, 0)) & (NT - 1)
    g = (m & (NT // 2 - 1)) - NT // 4
    x = g.astype(F32) * (2.0 * math.pi / NT)
    x2 = x * x
    acc = jnp.full(shape, SIN_TERMS[-1], F32)
    for term in SIN_TERMS[-2::-1]:
        acc = acc * x2 + term
    value = x * acc
    value = jnp.where(m >= NT // 2, value, -value)
    own = iota((shots, columns), 0) == iota((shots, columns), 1) % shots
    rows = [
        jnp.where(own, jnp.broadcast_to(value[j : j + 1], (shots, columns)), 0.0) for j in range(4)
    ]
    return jnp.concatenate(rows, axis=0).astype(BF16)


def kernel(
    n_wide, time_chunks,
    freq_ref, src_ref, aperture_ref, traces_ref, out_ref,
    x_ref, tx, rx, ctx, crx, stx, srx,
    load_sem, send_sem, recv_sem, csend_sem, crecv_sem, swap_sem,
):
    wide = lax.axis_index("wide")
    narrow = lax.axis_index("narrow")
    partner = 1 - narrow
    blocks, shots = aperture_ref.shape
    rows_total, receivers = traces_ref.shape
    rows = 4 * shots
    half = rows // 2
    recv_count = receivers // n_wide
    per_block = RB // recv_count
    sources = src_ref.shape[0]
    step = rows_total // time_chunks
    peers = n_wide - 1
    first = n_wide // 2

    def peer_of(i):
        return lax.rem(wide + 1 + lax.rem(first - 1 + i, peers), n_wide)

    def source_of(i):
        return lax.rem(wide + n_wide - 1 - lax.rem(first - 1 + i, peers), n_wide)

    barrier = pltpu.get_barrier_semaphore()
    each(peers, lambda i: pl.semaphore_signal(
        barrier, inc=1, device_id={"wide": peer_of(i)}, device_id_type=MESH))
    pl.semaphore_signal(barrier, inc=1, device_id={"narrow": partner}, device_id_type=MESH)

    loads = []
    for c in range(time_chunks):
        part = pl.ds(c * step, step)
        loads.append(pltpu.make_async_copy(traces_ref.at[part], x_ref.at[part], load_sem.at[c]))
        loads[-1].start()

    lane = iota((1, LANES), 1)
    lane_src = jnp.zeros((1, LANES), jnp.int32)
    for h in range(2):
        base = (narrow if h == 0 else partner) * shots
        for k in range(shots):
            at = (lane // rows == h) & (lane % shots == k)
            lane_src = jnp.where(at, src_ref[base + k], lane_src)
    first_time = wide * (rows_total // shots)
    tables = [dft_block(freq_ref, first_time, shots, step, c * step) for c in range(time_chunks)]

    low = iota((half, LANES), 1) < LANES // 2
    diagonal = iota((shots, shots), 0) == iota((shots, shots), 1)
    picked = None
    for b in range(blocks):
        raw = None
        for c in range(time_chunks):
            if b == 0:
                loads[c].wait()
            term = jnp.dot(
                tables[c],
                x_ref[c * step : (c + 1) * step, b * RB : (b + 1) * RB],
                preferred_element_type=F32,
            )
            raw = term if raw is None else raw + term
        flags = jnp.where(diagonal, aperture_ref[b : b + 1, :].astype(F32), 0.0)
        active = jnp.sum(flags, axis=1, keepdims=True) * NT ** (-0.5)
        spectra = raw * jnp.concatenate([active] * 4, axis=0)
        for p in range(per_block // 2):
            pair = spectra[:, p * LANES : (p + 1) * LANES]
            top, bottom = pair[:half], pair[half:]
            at = b * per_block + 2 * p
            tx[at] = jnp.where(low, top, pltpu.roll(bottom, LANES // 2, 1))
            tx[at + 1] = jnp.where(low, pltpu.roll(top, LANES // 2, 1), bottom)
        if b == blocks - 1:
            pl.semaphore_wait(barrier, peers + 1)

            def send(i):
                to = peer_of(i)
                pltpu.make_async_remote_copy(
                    src_ref=tx.at[to], dst_ref=rx.at[wide],
                    send_sem=send_sem.at[to], recv_sem=recv_sem.at[wide],
                    device_id={"wide": to}, device_id_type=MESH,
                ).start()

            each(peers, send)
        selector = (iota((RB, LANES), 0) + b * RB == lane_src).astype(F32).astype(BF16)
        hi = spectra.astype(BF16)
        rest = spectra - hi.astype(F32)
        mid = rest.astype(BF16)
        lo = (rest - mid.astype(F32)).astype(BF16)
        got = jnp.dot(jnp.concatenate([hi, mid, lo], axis=0), selector, preferred_element_type=F32)
        got = got[:rows] + got[rows : 2 * rows] + got[2 * rows :]
        picked = got if picked is None else picked + got

    kind = iota((shots, LANES), 1) // shots % 4
    packed = picked[:shots]
    for j in range(1, 4):
        packed = jnp.where(kind == j, picked[j * shots : (j + 1) * shots], packed)
    ctx[...] = packed

    def send_picked(i):
        to = peer_of(i)
        pltpu.make_async_remote_copy(
            src_ref=ctx, dst_ref=crx.at[wide],
            send_sem=csend_sem.at[to], recv_sem=crecv_sem.at[wide],
            device_id={"wide": to}, device_id_type=MESH,
        ).start()

    each(peers, send_picked)

    def copy_of(i):
        at = source_of(i)
        return pltpu.make_async_remote_copy(
            src_ref=tx.at[at], dst_ref=rx.at[at],
            send_sem=send_sem.at[at], recv_sem=recv_sem.at[at],
            device_id={"wide": at}, device_id_type=MESH,
        )

    def picked_copy_of(i):
        at = source_of(i)
        return pltpu.make_async_remote_copy(
            src_ref=ctx, dst_ref=crx.at[at],
            send_sem=csend_sem.at[at], recv_sem=crecv_sem.at[at],
            device_id={"wide": at}, device_id_type=MESH,
        )

    stx[...] = tx[wide]

    def add(i):
        copy_of(i).wait_recv()
        stx[...] += rx[source_of(i)]

    each(peers, add)
    swap = pltpu.make_async_remote_copy(
        src_ref=stx, dst_ref=srx, send_sem=swap_sem.at[0], recv_sem=swap_sem.at[1],
        device_id={"narrow": partner}, device_id_type=MESH,
    )
    swap.start()

    each(peers, lambda i: picked_copy_of(i).wait_recv())
    total = packed
    if peers <= 16:
        for i in range(peers):
            total = total + crx[source_of(i)]
    else:
        total = lax.fori_loop(0, peers, lambda i, c: c + crx[source_of(i)], total)
    total = total * sources ** (-0.5)
    quarter = LANES // 4
    part = iota((shots, LANES), 1) // quarter % 2
    swapped = jnp.where(
        part == 0, pltpu.roll(total, LANES - quarter, 1), pltpu.roll(total, quarter, 1)
    )
    signed = jnp.where(part == 0, total, -total)
    slice_of = iota((shots, LANES), 1) // shots % 2
    left = jnp.concatenate(
        [jnp.where(slice_of == q, v, 0.0) for v in (signed, swapped) for q in range(2)], axis=0
    )

    def spread(v):
        return jnp.concatenate([v[:, : LANES // 2], pltpu.roll(v, LANES // 2, 1)[:, : LANES // 2]], axis=0)

    result = jnp.dot(
        left[:, :rows], spread(stx[...]), preferred_element_type=F32, precision=lax.Precision.HIGHEST
    )
    swap.wait_recv()
    result = result + jnp.dot(
        left[:, rows:], spread(srx[...]), preferred_element_type=F32, precision=lax.Precision.HIGHEST
    )
    out_ref[...] = result.reshape(out_ref.shape)

    swap.wait_send()
    each(peers, lambda i: copy_of(i).wait_send())
    each(peers, lambda i: picked_copy_of(i).wait_send())


def solution(mesh):
    n_wide = mesh.shape["wide"]

    def shards(traces, aperture, source_points, freq_idx):
        times, shots, receivers = traces.shape
        recv_count = receivers // n_wide
        assert 2 * recv_count == LANES and 8 * shots == LANES
        assert mesh.shape["narrow"] == 2 and source_points.shape[0] == 2 * shots
        time_chunks = 4 if times % 32 == 0 else 1
        return pl.pallas_call(
            functools.partial(kernel, n_wide, time_chunks),
            out_shape=jax.ShapeDtypeStruct((2, 2, shots, recv_count), F32),
            in_specs=[
                pl.BlockSpec(memory_space=pltpu.SMEM),
                pl.BlockSpec(memory_space=pltpu.SMEM),
                pl.BlockSpec(memory_space=pltpu.VMEM),
                pl.BlockSpec(memory_space=pl.ANY),
            ],
            out_specs=pl.BlockSpec(memory_space=pltpu.VMEM),
            scratch_shapes=[
                pltpu.VMEM((times * shots, receivers), BF16),
                pltpu.VMEM((n_wide, 2 * shots, LANES), F32),
                pltpu.VMEM((n_wide, 2 * shots, LANES), F32),
                pltpu.VMEM((shots, LANES), F32),
                pltpu.VMEM((n_wide, shots, LANES), F32),
                pltpu.VMEM((2 * shots, LANES), F32),
                pltpu.VMEM((2 * shots, LANES), F32),
                pltpu.SemaphoreType.DMA((time_chunks,)),
                pltpu.SemaphoreType.DMA((n_wide,)),
                pltpu.SemaphoreType.DMA((n_wide,)),
                pltpu.SemaphoreType.DMA((n_wide,)),
                pltpu.SemaphoreType.DMA((n_wide,)),
                pltpu.SemaphoreType.DMA((2,)),
            ],
            compiler_params=pltpu.CompilerParams(
                collective_id=0, has_side_effects=True, vmem_limit_bytes=60 * 2**20
            ),
        )(freq_idx, source_points, aperture.T, traces.reshape(times * shots, receivers))

    placed = (P("wide", ("grp", "narrow"), None), P(("grp", "narrow"), None), P("grp"), P())
    return jax.shard_map(
        shards,
        mesh=mesh,
        in_specs=placed,
        out_specs=P(None, None, ("grp", "narrow"), "wide"),
        check_vma=False,
    )
```

```python
import functools
import math

import jax
import jax.numpy as jnp
from jax import lax
from jax.experimental import pallas as pl
from jax.experimental.pallas import tpu as pltpu
from jax.sharding import PartitionSpec as P

NT = 1024
RB = 512
LANES = 128
MESH = pl.DeviceIdType.MESH
F32 = jnp.float32
BF16 = jnp.bfloat16
SIN_TERMS = tuple((-1.0) ** i / math.factorial(2 * i + 1) for i in range(6))


def iota(shape, axis):
    return lax.broadcasted_iota(jnp.int32, shape, axis)


def each(count, body):
    if count <= 16:
        for i in range(count):
            body(i)
    else:
        lax.fori_loop(0, count, lambda i, c: (body(i), c)[1], 0)


def dft_block(freq_ref, first_time, shots, columns, first_column):
    shape = (8, columns)
    row = iota(shape, 0)
    lane = iota(shape, 1) + first_column
    freq = jnp.where(row % 2 == 0, freq_ref[0], freq_ref[1])
    m = freq * (first_time + lane // shots)
    m = (m + jnp.where(row >= 2, NT // 4, 0)) & (NT - 1)
    g = (m & (NT // 2 - 1)) - NT // 4
    x = g.astype(F32) * (2.0 * math.pi / NT)
    x2 = x * x
    acc = jnp.full(shape, SIN_TERMS[-1], F32)
    for term in SIN_TERMS[-2::-1]:
        acc = acc * x2 + term
    value = x * acc
    value = jnp.where(m >= NT // 2, value, -value)
    own = iota((shots, columns), 0) == iota((shots, columns), 1) % shots
    rows = [
        jnp.where(own, jnp.broadcast_to(value[j : j + 1], (shots, columns)), 0.0) for j in range(4)
    ]
    return jnp.concatenate(rows, axis=0).astype(BF16)


def kernel(
    n_wide, width,
    freq_hbm, src_hbm, aperture_hbm, traces_ref, out_ref,
    freq_ref, src_ref, aperture_ref, x_ref, tx, rx, ctx, crx, stx, srx,
    small_sem, load_sem, send_sem, recv_sem, csend_sem, crecv_sem, swap_sem,
):
    wide = lax.axis_index("wide")
    narrow = lax.axis_index("narrow")
    partner = 1 - narrow
    blocks, shots = aperture_ref.shape
    rows_total, receivers = traces_ref.shape
    rows = 4 * shots
    half = rows // 2
    recv_count = receivers // n_wide
    pieces = receivers // width
    peers = n_wide - 1

    def peer_of(i):
        return i + jnp.where(wide <= i, 1, 0)

    barrier = pltpu.get_barrier_semaphore()
    each(peers, lambda i: pl.semaphore_signal(
        barrier, inc=1, device_id={"wide": peer_of(i)}, device_id_type=MESH))
    pl.semaphore_signal(barrier, inc=1, device_id={"narrow": partner}, device_id_type=MESH)

    smalls = [
        pltpu.make_async_copy(here, there, small_sem.at[i])
        for i, (here, there) in enumerate(
            ((freq_hbm, freq_ref), (src_hbm, src_ref), (aperture_hbm, aperture_ref))
        )
    ]
    for copy in smalls:
        copy.start()
    loads = [
        pltpu.make_async_copy(
            traces_ref.at[:, pl.ds(c * width, width)], x_ref.at[c], load_sem.at[c]
        )
        for c in range(pieces)
    ]
    for copy in loads:
        copy.start()
    for copy in smalls:
        copy.wait()

    lane = iota((1, LANES), 1)
    lane_src = jnp.zeros((1, LANES), jnp.int32)
    for h in range(2):
        base = (narrow if h == 0 else partner) * shots
        for k in range(shots):
            at = (lane // rows == h) & (lane % shots == k)
            lane_src = jnp.where(at, src_ref[base + k], lane_src)
    first_time = wide * (rows_total // shots)
    table = dft_block(freq_ref, first_time, shots, rows_total, 0)

    low = iota((half, LANES), 1) < LANES // 2
    diagonal = iota((shots, shots), 0) == iota((shots, shots), 1)
    picked = None
    def send(to):
        @pl.when(to != wide)
        def _():
            pltpu.make_async_remote_copy(
                src_ref=tx.at[to], dst_ref=rx.at[wide],
                send_sem=send_sem.at[to], recv_sem=recv_sem.at[wide],
                device_id={"wide": to}, device_id_type=MESH,
            ).start()

    def active_of(b):
        flags = jnp.where(diagonal, aperture_ref[b : b + 1, :].astype(F32), 0.0)
        active = jnp.sum(flags, axis=1, keepdims=True) * NT ** (-0.5)
        return jnp.concatenate([active] * 4, axis=0)

    actives = [active_of(b) for b in range(blocks)]
    for c in range(pieces):
        loads[c].wait()
        raw = jnp.dot(table, x_ref[c], preferred_element_type=F32)
        spectra = raw * actives[c * width // RB]
        per_piece = width // recv_count
        for p in range(per_piece // 2):
            pair = spectra[:, p * LANES : (p + 1) * LANES]
            top, bottom = pair[:half], pair[half:]
            at = c * per_piece + 2 * p
            tx[at] = jnp.where(low, top, pltpu.roll(bottom, LANES // 2, 1))
            tx[at + 1] = jnp.where(low, pltpu.roll(top, LANES // 2, 1), bottom)
        if c == 0:
            pl.semaphore_wait(barrier, peers + 1)
        each(per_piece, lambda i: send(c * per_piece + i))
        selector = (iota((width, LANES), 0) + c * width == lane_src).astype(F32).astype(BF16)
        hi = spectra.astype(BF16)
        rest = spectra - hi.astype(F32)
        mid = rest.astype(BF16)
        lo = (rest - mid.astype(F32)).astype(BF16)
        got = jnp.dot(jnp.concatenate([hi, mid, lo], axis=0), selector, preferred_element_type=F32)
        got = got[:rows] + got[rows : 2 * rows] + got[2 * rows :]
        picked = got if picked is None else picked + got

    kind = iota((shots, LANES), 1) // shots % 4
    packed = picked[:shots]
    for j in range(1, 4):
        packed = jnp.where(kind == j, picked[j * shots : (j + 1) * shots], packed)
    ctx[...] = packed

    def send_picked(i):
        to = peer_of(i)
        pltpu.make_async_remote_copy(
            src_ref=ctx, dst_ref=crx.at[wide],
            send_sem=csend_sem.at[to], recv_sem=crecv_sem.at[wide],
            device_id={"wide": to}, device_id_type=MESH,
        ).start()

    each(peers, send_picked)

    def copy_of(i):
        at = peer_of(i)
        return pltpu.make_async_remote_copy(
            src_ref=tx.at[at], dst_ref=rx.at[at],
            send_sem=send_sem.at[at], recv_sem=recv_sem.at[at],
            device_id={"wide": at}, device_id_type=MESH,
        )

    def picked_copy_of(i):
        at = peer_of(i)
        return pltpu.make_async_remote_copy(
            src_ref=ctx, dst_ref=crx.at[at],
            send_sem=csend_sem.at[at], recv_sem=crecv_sem.at[at],
            device_id={"wide": at}, device_id_type=MESH,
        )

    stx[...] = tx[wide]

    def add(i):
        copy_of(i).wait_recv()
        stx[...] += rx[peer_of(i)]

    each(peers, add)
    swap = pltpu.make_async_remote_copy(
        src_ref=stx, dst_ref=srx, send_sem=swap_sem.at[0], recv_sem=swap_sem.at[1],
        device_id={"narrow": partner}, device_id_type=MESH,
    )
    swap.start()

    each(peers, lambda i: picked_copy_of(i).wait_recv())
    total = packed
    if peers <= 16:
        for i in range(peers):
            total = total + crx[peer_of(i)]
    else:
        total = lax.fori_loop(0, peers, lambda i, c: c + crx[peer_of(i)], total)
    quarter = LANES // 4
    part = iota((shots, LANES), 1) // quarter % 2
    swapped = jnp.where(
        part == 0, pltpu.roll(total, LANES - quarter, 1), pltpu.roll(total, quarter, 1)
    )
    signed = jnp.where(part == 0, total, -total)
    slice_of = iota((shots, LANES), 1) // shots % 2
    left = jnp.concatenate(
        [jnp.where(slice_of == q, v, 0.0) for v in (signed, swapped) for q in range(2)], axis=0
    )

    def spread(v):
        return jnp.concatenate([v[:, : LANES // 2], pltpu.roll(v, LANES // 2, 1)[:, : LANES // 2]], axis=0)

    result = jnp.dot(
        left[:, :rows], spread(stx[...]), preferred_element_type=F32, precision=lax.Precision.HIGHEST
    )
    swap.wait_recv()
    result = result + jnp.dot(
        left[:, rows:], spread(srx[...]), preferred_element_type=F32, precision=lax.Precision.HIGHEST
    )
    out_ref[...] = result.reshape(out_ref.shape)

    swap.wait_send()
    each(peers, lambda i: copy_of(i).wait_send())
    each(peers, lambda i: picked_copy_of(i).wait_send())


def solution(mesh):
    n_wide = mesh.shape["wide"]

    def shards(traces, aperture, source_points, freq_idx):
        times, shots, receivers = traces.shape
        recv_count = receivers // n_wide
        assert 2 * recv_count == LANES and 8 * shots == LANES
        assert mesh.shape["narrow"] == 2 and source_points.shape[0] == 2 * shots
        width = LANES if n_wide <= 16 else RB
        pieces = receivers // width
        products = pl.pallas_call(
            functools.partial(kernel, n_wide, width),
            out_shape=pltpu.VMEM((2, 2, shots, recv_count), F32),
            in_specs=[pl.BlockSpec(memory_space=pltpu.HBM)] * 4,
            out_specs=pl.BlockSpec(memory_space=pltpu.VMEM),
            scratch_shapes=[
                pltpu.SMEM(freq_idx.shape, jnp.int32),
                pltpu.SMEM(source_points.shape, jnp.int32),
                pltpu.VMEM(aperture.shape[::-1], jnp.int32),
                pltpu.VMEM((pieces, times * shots, width), BF16),
                pltpu.VMEM((n_wide, 2 * shots, LANES), F32),
                pltpu.VMEM((n_wide, 2 * shots, LANES), F32),
                pltpu.VMEM((shots, LANES), F32),
                pltpu.VMEM((n_wide, shots, LANES), F32),
                pltpu.VMEM((2 * shots, LANES), F32),
                pltpu.VMEM((2 * shots, LANES), F32),
                pltpu.SemaphoreType.DMA((3,)),
                pltpu.SemaphoreType.DMA((pieces,)),
                pltpu.SemaphoreType.DMA((n_wide,)),
                pltpu.SemaphoreType.DMA((n_wide,)),
                pltpu.SemaphoreType.DMA((n_wide,)),
                pltpu.SemaphoreType.DMA((n_wide,)),
                pltpu.SemaphoreType.DMA((2,)),
            ],
            compiler_params=pltpu.CompilerParams(
                collective_id=0, has_side_effects=True, vmem_limit_bytes=60 * 2**20
            ),
        )(freq_idx, source_points, aperture.T, traces.reshape(times * shots, receivers))
        return products * source_points.shape[0] ** (-0.5)

    placed = (P("wide", ("grp", "narrow"), None), P(("grp", "narrow"), None), P("grp"), P())
    return jax.shard_map(
        shards,
        mesh=mesh,
        in_specs=placed,
        out_specs=P(None, None, ("grp", "narrow"), "wide"),
        check_vma=False,
    )
```

```python
import functools
import math

import jax
import jax.numpy as jnp
from jax import lax
from jax.experimental import pallas as pl
from jax.experimental.pallas import tpu as pltpu
from jax.sharding import PartitionSpec as P

NT = 1024
RB = 512
LANES = 128
MESH = pl.DeviceIdType.MESH
F32 = jnp.float32
BF16 = jnp.bfloat16
SIN_TERMS = tuple((-1.0) ** i / math.factorial(2 * i + 1) for i in range(6))


def iota(shape, axis):
    return lax.broadcasted_iota(jnp.int32, shape, axis)


def each(count, body):
    if count <= 16:
        for i in range(count):
            body(i)
    else:
        lax.fori_loop(0, count, lambda i, c: (body(i), c)[1], 0)


def dft_block(freq_ref, first_time, shots, columns, first_column):
    shape = (8, columns)
    row = iota(shape, 0)
    lane = iota(shape, 1) + first_column
    freq = jnp.where(row % 2 == 0, freq_ref[0], freq_ref[1])
    m = freq * (first_time + lane // shots)
    m = (m + jnp.where(row >= 2, NT // 4, 0)) & (NT - 1)
    g = (m & (NT // 2 - 1)) - NT // 4
    x = g.astype(F32) * (2.0 * math.pi / NT)
    x2 = x * x
    acc = jnp.full(shape, SIN_TERMS[-1], F32)
    for term in SIN_TERMS[-2::-1]:
        acc = acc * x2 + term
    value = x * acc
    value = jnp.where(m >= NT // 2, value, -value)
    own = iota((shots, columns), 0) == iota((shots, columns), 1) % shots
    rows = [
        jnp.where(own, jnp.broadcast_to(value[j : j + 1], (shots, columns)), 0.0) for j in range(4)
    ]
    return jnp.concatenate(rows, axis=0).astype(BF16)


def kernel(
    n_wide, width,
    freq_hbm, src_hbm, aperture_hbm, traces_ref, out_ref,
    freq_ref, src_ref, aperture_ref, x_ref, tx, rx, ctx, crx, stx, srx,
    small_sem, load_sem, send_sem, recv_sem, csend_sem, crecv_sem, swap_sem, ready_sem,
):
    wide = lax.axis_index("wide")
    narrow = lax.axis_index("narrow")
    partner = 1 - narrow
    blocks, shots = aperture_ref.shape
    rows_total, receivers = traces_ref.shape
    rows = 4 * shots
    half = rows // 2
    recv_count = receivers // n_wide
    pieces = receivers // width
    peers = n_wide - 1

    def peer_of(i):
        return i + jnp.where(wide <= i, 1, 0)

    barrier = pltpu.get_barrier_semaphore()

    def announce(to):
        @pl.when(to > wide)
        def _():
            pl.semaphore_signal(barrier, inc=1, device_id={"wide": to}, device_id_type=MESH)

    def answer(to):
        @pl.when(to < wide)
        def _():
            pl.semaphore_signal(
                ready_sem.at[wide], inc=1, device_id={"wide": to}, device_id_type=MESH
            )

    each(n_wide, announce)
    pl.semaphore_signal(barrier, inc=1, device_id={"narrow": partner}, device_id_type=MESH)

    smalls = [
        pltpu.make_async_copy(here, there, small_sem.at[i])
        for i, (here, there) in enumerate(
            ((freq_hbm, freq_ref), (src_hbm, src_ref), (aperture_hbm, aperture_ref))
        )
    ]
    for copy in smalls:
        copy.start()
    loads = [
        pltpu.make_async_copy(
            traces_ref.at[:, pl.ds(c * width, width)], x_ref.at[c], load_sem.at[c]
        )
        for c in range(pieces)
    ]
    for copy in loads:
        copy.start()
    pl.semaphore_wait(barrier, wide + 1)
    each(n_wide, answer)
    for copy in smalls:
        copy.wait()

    lane = iota((1, LANES), 1)
    lane_src = jnp.zeros((1, LANES), jnp.int32)
    for h in range(2):
        base = (narrow if h == 0 else partner) * shots
        for k in range(shots):
            at = (lane // rows == h) & (lane % shots == k)
            lane_src = jnp.where(at, src_ref[base + k], lane_src)
    first_time = wide * (rows_total // shots)
    table = dft_block(freq_ref, first_time, shots, rows_total, 0)

    low = iota((half, LANES), 1) < LANES // 2
    diagonal = iota((shots, shots), 0) == iota((shots, shots), 1)
    picked = None
    def spectra_to(to):
        return pltpu.make_async_remote_copy(
            src_ref=tx.at[to], dst_ref=rx.at[wide],
            send_sem=send_sem.at[to], recv_sem=recv_sem.at[wide],
            device_id={"wide": to}, device_id_type=MESH,
        )

    def send_below(to):
        @pl.when(to < wide)
        def _():
            spectra_to(to).start()

    def active_of(b):
        flags = jnp.where(diagonal, aperture_ref[b : b + 1, :].astype(F32), 0.0)
        active = jnp.sum(flags, axis=1, keepdims=True) * NT ** (-0.5)
        return jnp.concatenate([active] * 4, axis=0)

    actives = [active_of(b) for b in range(blocks)]
    for c in range(pieces):
        loads[c].wait()
        raw = jnp.dot(table, x_ref[c], preferred_element_type=F32)
        spectra = raw * actives[c * width // RB]
        per_piece = width // recv_count
        for p in range(per_piece // 2):
            pair = spectra[:, p * LANES : (p + 1) * LANES]
            top, bottom = pair[:half], pair[half:]
            at = c * per_piece + 2 * p
            tx[at] = jnp.where(low, top, pltpu.roll(bottom, LANES // 2, 1))
            tx[at + 1] = jnp.where(low, pltpu.roll(top, LANES // 2, 1), bottom)
        if c == 0:
            each(per_piece, send_below)
        selector = (iota((width, LANES), 0) + c * width == lane_src).astype(F32).astype(BF16)
        hi = spectra.astype(BF16)
        rest = spectra - hi.astype(F32)
        mid = rest.astype(BF16)
        lo = (rest - mid.astype(F32)).astype(BF16)
        got = jnp.dot(jnp.concatenate([hi, mid, lo], axis=0), selector, preferred_element_type=F32)
        got = got[:rows] + got[rows : 2 * rows] + got[2 * rows :]
        picked = got if picked is None else picked + got

    kind = iota((shots, LANES), 1) // shots % 4
    packed = picked[:shots]
    for j in range(1, 4):
        packed = jnp.where(kind == j, picked[j * shots : (j + 1) * shots], packed)
    ctx[...] = packed

    def send_rest(i):
        to = peer_of(i)

        @pl.when(to > wide)
        def _():
            pl.semaphore_wait(ready_sem.at[to], 1)

        @pl.when((to > wide) | (to >= width // recv_count))
        def _():
            spectra_to(to).start()

        pltpu.make_async_remote_copy(
            src_ref=ctx, dst_ref=crx.at[wide],
            send_sem=csend_sem.at[to], recv_sem=crecv_sem.at[wide],
            device_id={"wide": to}, device_id_type=MESH,
        ).start()

    each(peers, send_rest)

    def copy_of(i):
        at = peer_of(i)
        return pltpu.make_async_remote_copy(
            src_ref=tx.at[at], dst_ref=rx.at[at],
            send_sem=send_sem.at[at], recv_sem=recv_sem.at[at],
            device_id={"wide": at}, device_id_type=MESH,
        )

    def picked_copy_of(i):
        at = peer_of(i)
        return pltpu.make_async_remote_copy(
            src_ref=ctx, dst_ref=crx.at[at],
            send_sem=csend_sem.at[at], recv_sem=crecv_sem.at[at],
            device_id={"wide": at}, device_id_type=MESH,
        )

    stx[...] = tx[wide]

    def add(i):
        copy_of(i).wait_recv()
        stx[...] += rx[peer_of(i)]

    each(peers, add)
    swap = pltpu.make_async_remote_copy(
        src_ref=stx, dst_ref=srx, send_sem=swap_sem.at[0], recv_sem=swap_sem.at[1],
        device_id={"narrow": partner}, device_id_type=MESH,
    )
    swap.start()

    each(peers, lambda i: picked_copy_of(i).wait_recv())
    total = packed
    if peers <= 16:
        for i in range(peers):
            total = total + crx[peer_of(i)]
    else:
        total = lax.fori_loop(0, peers, lambda i, c: c + crx[peer_of(i)], total)
    quarter = LANES // 4
    part = iota((shots, LANES), 1) // quarter % 2
    swapped = jnp.where(
        part == 0, pltpu.roll(total, LANES - quarter, 1), pltpu.roll(total, quarter, 1)
    )
    signed = jnp.where(part == 0, total, -total)
    slice_of = iota((shots, LANES), 1) // shots % 2
    left = jnp.concatenate(
        [jnp.where(slice_of == q, v, 0.0) for v in (signed, swapped) for q in range(2)], axis=0
    )

    def spread(v):
        return jnp.concatenate([v[:, : LANES // 2], pltpu.roll(v, LANES // 2, 1)[:, : LANES // 2]], axis=0)

    result = jnp.dot(
        left[:, :rows], spread(stx[...]), preferred_element_type=F32, precision=lax.Precision.HIGHEST
    )
    swap.wait_recv()
    result = result + jnp.dot(
        left[:, rows:], spread(srx[...]), preferred_element_type=F32, precision=lax.Precision.HIGHEST
    )
    out_ref[...] = result.reshape(out_ref.shape)

    swap.wait_send()
    each(peers, lambda i: copy_of(i).wait_send())
    each(peers, lambda i: picked_copy_of(i).wait_send())


def solution(mesh):
    n_wide = mesh.shape["wide"]

    def shards(traces, aperture, source_points, freq_idx):
        times, shots, receivers = traces.shape
        recv_count = receivers // n_wide
        assert 2 * recv_count == LANES and 8 * shots == LANES
        assert mesh.shape["narrow"] == 2 and source_points.shape[0] == 2 * shots
        width = LANES if n_wide <= 16 else RB
        pieces = receivers // width
        products = pl.pallas_call(
            functools.partial(kernel, n_wide, width),
            out_shape=pltpu.VMEM((2, 2, shots, recv_count), F32),
            in_specs=[pl.BlockSpec(memory_space=pltpu.HBM)] * 4,
            out_specs=pl.BlockSpec(memory_space=pltpu.VMEM),
            scratch_shapes=[
                pltpu.SMEM(freq_idx.shape, jnp.int32),
                pltpu.SMEM(source_points.shape, jnp.int32),
                pltpu.VMEM(aperture.shape[::-1], jnp.int32),
                pltpu.VMEM((pieces, times * shots, width), BF16),
                pltpu.VMEM((n_wide, 2 * shots, LANES), F32),
                pltpu.VMEM((n_wide, 2 * shots, LANES), F32),
                pltpu.VMEM((shots, LANES), F32),
                pltpu.VMEM((n_wide, shots, LANES), F32),
                pltpu.VMEM((2 * shots, LANES), F32),
                pltpu.VMEM((2 * shots, LANES), F32),
                pltpu.SemaphoreType.DMA((3,)),
                pltpu.SemaphoreType.DMA((pieces,)),
                pltpu.SemaphoreType.DMA((n_wide,)),
                pltpu.SemaphoreType.DMA((n_wide,)),
                pltpu.SemaphoreType.DMA((n_wide,)),
                pltpu.SemaphoreType.DMA((n_wide,)),
                pltpu.SemaphoreType.DMA((2,)),
                pltpu.SemaphoreType.REGULAR((n_wide,)),
            ],
            compiler_params=pltpu.CompilerParams(
                collective_id=0, has_side_effects=True, vmem_limit_bytes=60 * 2**20
            ),
        )(freq_idx, source_points, aperture.T, traces.reshape(times * shots, receivers))
        return products * source_points.shape[0] ** (-0.5)

    placed = (P("wide", ("grp", "narrow"), None), P(("grp", "narrow"), None), P("grp"), P())
    return jax.shard_map(
        shards,
        mesh=mesh,
        in_specs=placed,
        out_specs=P(None, None, ("grp", "narrow"), "wide"),
        check_vma=False,
    )
```

```python
import functools
import math

import jax
import jax.numpy as jnp
from jax import lax
from jax.experimental import pallas as pl
from jax.experimental.pallas import tpu as pltpu
from jax.sharding import PartitionSpec as P

NT = 1024
RB = 512
LANES = 128
MESH = pl.DeviceIdType.MESH
F32 = jnp.float32
BF16 = jnp.bfloat16
SIN_TERMS = tuple((-1.0) ** i / math.factorial(2 * i + 1) for i in range(6))


def iota(shape, axis):
    return lax.broadcasted_iota(jnp.int32, shape, axis)


def each(count, body):
    if count <= 16:
        for i in range(count):
            body(i)
    else:
        lax.fori_loop(0, count, lambda i, c: (body(i), c)[1], 0)


def dft_block(freq_ref, first_time, shots, columns, first_column):
    shape = (8, columns)
    row = iota(shape, 0)
    lane = iota(shape, 1) + first_column
    freq = jnp.where(row % 2 == 0, freq_ref[0], freq_ref[1])
    m = freq * (first_time + lane // shots)
    m = (m + jnp.where(row >= 2, NT // 4, 0)) & (NT - 1)
    g = (m & (NT // 2 - 1)) - NT // 4
    x = g.astype(F32) * (2.0 * math.pi / NT)
    x2 = x * x
    acc = jnp.full(shape, SIN_TERMS[-1], F32)
    for term in SIN_TERMS[-2::-1]:
        acc = acc * x2 + term
    value = x * acc
    value = jnp.where(m >= NT // 2, value, -value)
    own = iota((shots, columns), 0) == iota((shots, columns), 1) % shots
    rows = [
        jnp.where(own, jnp.broadcast_to(value[j : j + 1], (shots, columns)), 0.0) for j in range(4)
    ]
    return jnp.concatenate(rows, axis=0).astype(BF16)


def kernel(
    n_wide, width,
    freq_hbm, src_hbm, aperture_hbm, traces_ref, out_ref,
    freq_ref, src_ref, aperture_ref, x_ref, tx, rx, ctx, crx, stx, srx,
    small_sem, load_sem, send_sem, recv_sem, csend_sem, crecv_sem, swap_sem, ready_sem,
):
    wide = lax.axis_index("wide")
    narrow = lax.axis_index("narrow")
    partner = 1 - narrow
    blocks, shots = aperture_ref.shape
    rows_total, receivers = traces_ref.shape
    rows = 4 * shots
    half = rows // 2
    recv_count = receivers // n_wide
    pieces = receivers // width
    peers = n_wide - 1

    def peer_of(i):
        return i + jnp.where(wide <= i, 1, 0)

    barrier = pltpu.get_barrier_semaphore()

    def announce(to):
        @pl.when(to > wide)
        def _():
            pl.semaphore_signal(barrier, inc=1, device_id={"wide": to}, device_id_type=MESH)

    def answer(to):
        @pl.when(to < wide)
        def _():
            pl.semaphore_signal(
                ready_sem.at[wide], inc=1, device_id={"wide": to}, device_id_type=MESH
            )

    each(n_wide, announce)
    pl.semaphore_signal(barrier, inc=1, device_id={"narrow": partner}, device_id_type=MESH)

    smalls = [
        pltpu.make_async_copy(here, there, small_sem.at[i])
        for i, (here, there) in enumerate(
            ((freq_hbm, freq_ref), (src_hbm, src_ref), (aperture_hbm, aperture_ref))
        )
    ]
    for copy in smalls:
        copy.start()
    deep = rows_total // 2
    loads = [
        pltpu.make_async_copy(
            traces_ref.at[pl.ds(r * deep, deep), pl.ds(c * width, width)],
            x_ref.at[c, pl.ds(r * deep, deep)],
            load_sem.at[2 * c + r],
        )
        for c in range(pieces)
        for r in range(2)
    ]
    for copy in loads:
        copy.start()
    pl.semaphore_wait(barrier, wide + 1)
    each(n_wide, answer)
    for copy in smalls:
        copy.wait()

    lane = iota((1, LANES), 1)
    lane_src = jnp.zeros((1, LANES), jnp.int32)
    for h in range(2):
        base = (narrow if h == 0 else partner) * shots
        for k in range(shots):
            at = (lane // rows == h) & (lane % shots == k)
            lane_src = jnp.where(at, src_ref[base + k], lane_src)
    first_time = wide * (rows_total // shots)
    table = dft_block(freq_ref, first_time, shots, rows_total, 0)

    low = iota((half, LANES), 1) < LANES // 2
    diagonal = iota((shots, shots), 0) == iota((shots, shots), 1)
    picked = None
    def spectra_to(to):
        return pltpu.make_async_remote_copy(
            src_ref=tx.at[to], dst_ref=rx.at[wide],
            send_sem=send_sem.at[to], recv_sem=recv_sem.at[wide],
            device_id={"wide": to}, device_id_type=MESH,
        )

    def send_below(to):
        @pl.when(to < wide)
        def _():
            spectra_to(to).start()

    def active_of(b):
        flags = jnp.where(diagonal, aperture_ref[b : b + 1, :].astype(F32), 0.0)
        active = jnp.sum(flags, axis=1, keepdims=True) * NT ** (-0.5)
        return jnp.concatenate([active] * 4, axis=0)

    actives = [active_of(b) for b in range(blocks)]
    for c in range(pieces):
        loads[2 * c].wait()
        loads[2 * c + 1].wait()
        raw = jnp.dot(table, x_ref[c], preferred_element_type=F32)
        spectra = raw * actives[c * width // RB]
        per_piece = width // recv_count
        for p in range(per_piece // 2):
            pair = spectra[:, p * LANES : (p + 1) * LANES]
            top, bottom = pair[:half], pair[half:]
            at = c * per_piece + 2 * p
            tx[at] = jnp.where(low, top, pltpu.roll(bottom, LANES // 2, 1))
            tx[at + 1] = jnp.where(low, pltpu.roll(top, LANES // 2, 1), bottom)
        if c == 0:
            each(per_piece, send_below)
        selector = (iota((width, LANES), 0) + c * width == lane_src).astype(F32).astype(BF16)
        hi = spectra.astype(BF16)
        rest = spectra - hi.astype(F32)
        mid = rest.astype(BF16)
        lo = (rest - mid.astype(F32)).astype(BF16)
        got = jnp.dot(jnp.concatenate([hi, mid, lo], axis=0), selector, preferred_element_type=F32)
        got = got[:rows] + got[rows : 2 * rows] + got[2 * rows :]
        picked = got if picked is None else picked + got

    kind = iota((shots, LANES), 1) // shots % 4
    packed = picked[:shots]
    for j in range(1, 4):
        packed = jnp.where(kind == j, picked[j * shots : (j + 1) * shots], packed)
    ctx[...] = packed

    def send_rest(i):
        to = peer_of(i)

        @pl.when(to > wide)
        def _():
            pl.semaphore_wait(ready_sem.at[to], 1)

        @pl.when((to > wide) | (to >= width // recv_count))
        def _():
            spectra_to(to).start()

        pltpu.make_async_remote_copy(
            src_ref=ctx, dst_ref=crx.at[wide],
            send_sem=csend_sem.at[to], recv_sem=crecv_sem.at[wide],
            device_id={"wide": to}, device_id_type=MESH,
        ).start()

    each(peers, send_rest)

    def copy_of(i):
        at = peer_of(i)
        return pltpu.make_async_remote_copy(
            src_ref=tx.at[at], dst_ref=rx.at[at],
            send_sem=send_sem.at[at], recv_sem=recv_sem.at[at],
            device_id={"wide": at}, device_id_type=MESH,
        )

    def picked_copy_of(i):
        at = peer_of(i)
        return pltpu.make_async_remote_copy(
            src_ref=ctx, dst_ref=crx.at[at],
            send_sem=csend_sem.at[at], recv_sem=crecv_sem.at[at],
            device_id={"wide": at}, device_id_type=MESH,
        )

    stx[...] = tx[wide]

    def add(i):
        copy_of(i).wait_recv()
        stx[...] += rx[peer_of(i)]

    each(peers, add)
    swap = pltpu.make_async_remote_copy(
        src_ref=stx, dst_ref=srx, send_sem=swap_sem.at[0], recv_sem=swap_sem.at[1],
        device_id={"narrow": partner}, device_id_type=MESH,
    )
    swap.start()

    each(peers, lambda i: picked_copy_of(i).wait_recv())
    total = packed
    if peers <= 16:
        for i in range(peers):
            total = total + crx[peer_of(i)]
    else:
        total = lax.fori_loop(0, peers, lambda i, c: c + crx[peer_of(i)], total)
    quarter = LANES // 4
    part = iota((shots, LANES), 1) // quarter % 2
    swapped = jnp.where(
        part == 0, pltpu.roll(total, LANES - quarter, 1), pltpu.roll(total, quarter, 1)
    )
    signed = jnp.where(part == 0, total, -total)
    slice_of = iota((shots, LANES), 1) // shots % 2
    left = jnp.concatenate(
        [jnp.where(slice_of == q, v, 0.0) for v in (signed, swapped) for q in range(2)], axis=0
    )

    def spread(v):
        return jnp.concatenate([v[:, : LANES // 2], pltpu.roll(v, LANES // 2, 1)[:, : LANES // 2]], axis=0)

    result = jnp.dot(
        left[:, :rows], spread(stx[...]), preferred_element_type=F32, precision=lax.Precision.HIGHEST
    )
    swap.wait_recv()
    result = result + jnp.dot(
        left[:, rows:], spread(srx[...]), preferred_element_type=F32, precision=lax.Precision.HIGHEST
    )
    out_ref[...] = result.reshape(out_ref.shape)

    swap.wait_send()
    each(peers, lambda i: copy_of(i).wait_send())
    each(peers, lambda i: picked_copy_of(i).wait_send())


def solution(mesh):
    n_wide = mesh.shape["wide"]

    def shards(traces, aperture, source_points, freq_idx):
        times, shots, receivers = traces.shape
        recv_count = receivers // n_wide
        assert 2 * recv_count == LANES and 8 * shots == LANES
        assert mesh.shape["narrow"] == 2 and source_points.shape[0] == 2 * shots
        width = LANES if n_wide <= 16 else RB
        pieces = receivers // width
        products = pl.pallas_call(
            functools.partial(kernel, n_wide, width),
            out_shape=pltpu.VMEM((2, 2, shots, recv_count), F32),
            in_specs=[pl.BlockSpec(memory_space=pltpu.HBM)] * 4,
            out_specs=pl.BlockSpec(memory_space=pltpu.VMEM),
            scratch_shapes=[
                pltpu.SMEM(freq_idx.shape, jnp.int32),
                pltpu.SMEM(source_points.shape, jnp.int32),
                pltpu.VMEM(aperture.shape[::-1], jnp.int32),
                pltpu.VMEM((pieces, times * shots, width), BF16),
                pltpu.VMEM((n_wide, 2 * shots, LANES), F32),
                pltpu.VMEM((n_wide, 2 * shots, LANES), F32),
                pltpu.VMEM((shots, LANES), F32),
                pltpu.VMEM((n_wide, shots, LANES), F32),
                pltpu.VMEM((2 * shots, LANES), F32),
                pltpu.VMEM((2 * shots, LANES), F32),
                pltpu.SemaphoreType.DMA((3,)),
                pltpu.SemaphoreType.DMA((2 * pieces,)),
                pltpu.SemaphoreType.DMA((n_wide,)),
                pltpu.SemaphoreType.DMA((n_wide,)),
                pltpu.SemaphoreType.DMA((n_wide,)),
                pltpu.SemaphoreType.DMA((n_wide,)),
                pltpu.SemaphoreType.DMA((2,)),
                pltpu.SemaphoreType.REGULAR((n_wide,)),
            ],
            compiler_params=pltpu.CompilerParams(
                collective_id=0, has_side_effects=True, vmem_limit_bytes=60 * 2**20
            ),
        )(freq_idx, source_points, aperture.T, traces.reshape(times * shots, receivers))
        return products * source_points.shape[0] ** (-0.5)

    placed = (P("wide", ("grp", "narrow"), None), P(("grp", "narrow"), None), P("grp"), P())
    return jax.shard_map(
        shards,
        mesh=mesh,
        in_specs=placed,
        out_specs=P(None, None, ("grp", "narrow"), "wide"),
        check_vma=False,
    )
```
